32 devices in a mesh: row: 4 (over z), col: 8 (over y, x, core).
Axes of the slice: x: 2, y: 2, z: 4, core: 2. Of those that a mesh axis runs over, the one named last changes fastest.
Arguments:
- layer_input: bfloat16 [1024, 12288], P('col', 'row'), may hold values from -6 to 6
- heads_output: bfloat16 [1024, 6144], P('row', 'col'), may hold values from -6 to 6
- query_cot: bfloat16 [1024, 6144], P('row', 'col'), may hold values from -0.83984375 to 0.83984375
- keyval_cot: bfloat16 [1024, 1024], P('col'), may hold values from -0.83984375 to 0.83984375
- output_cot: bfloat16 [1024, 12288], P('col', 'row'), may hold values from -0.83984375 to 0.83984375
- query_weight: bfloat16 [12288, 6144], P('row', 'col'), may hold values from -0.0546875 to 0.0546875
- keyval_weight: bfloat16 [12288, 1024], P('row'), may hold values from -0.0546875 to 0.0546875
- out_weight: bfloat16 [6144, 12288], P('col', 'row'), may hold values from -0.078125 to 0.078125
Outputs:
- input_grad: bfloat16 [1024, 12288], P('col', 'row')
- heads_grad: bfloat16 [1024, 6144], P('row', 'col')
- query_wgrad: bfloat16 [12288, 6144], P('row', 'col')
- keyval_wgrad: bfloat16 [12288, 1024], P('row')
- out_wgrad: bfloat16 [6144, 12288], P('col', 'row')
The draws below stay inside these ranges and needn't reach their ends.
All inputs are finite; a program needn't handle non-finite values.
Results may differ from the reference program's by a relative error of at most 0.001.
Values may be sent and summed in bfloat16 or wider, within the bound.
A program may use at most 192 MiB of HBM per device.

```python
import jax
import jax.numpy as jnp

D = 12288
TOKENS = 1024
F = 6144
G = 1024


def shard_levels(rng, dims, shards, least, largest):
    def one(dim, shards_of):
        steps = jax.random.uniform(jax.random.fold_in(jax.random.fold_in(rng, 6), dim), (shards_of,), jnp.float32, least / len(shards), largest / len(shards))
        return jnp.repeat(jnp.exp(steps), dims[dim] // shards_of).reshape((-1,) + (1,) * (len(dims) - dim - 1))

    factor_of = one(*shards[0])
    for cut in shards[1:]:
        factor_of = factor_of * one(*cut)
    return factor_of


def scatter_about(key, extent, deviation, reach, pieces=(), kind=jnp.bfloat16):
    values = jax.random.normal(key, extent, jnp.float32) * deviation
    if len(pieces) > 0:
        values = shard_levels(key, extent, pieces, -0.22, 0.18) * values
    return jnp.clip(values, min=-reach, max=reach).astype(kind)


def setup_inputs(seed: int = 0) -> dict:
    streams_of = jax.random.split(jax.random.key(seed), 9)
    layer_input = scatter_about(streams_of[0], (TOKENS, D), 1.0, 6.0, ((0, 8), (1, 4)))
    heads_output = scatter_about(streams_of[1], (TOKENS, F), 1.0, 6.0, ((0, 4), (1, 8)))
    query_cot = scatter_about(streams_of[2], (TOKENS, F), 0.14, 0.83984375, ((0, 4), (1, 8)))
    keyval_cot = scatter_about(streams_of[3], (TOKENS, G), 0.14, 0.83984375, ((0, 8),))
    output_cot = scatter_about(streams_of[4], (TOKENS, D), 0.14, 0.83984375, ((0, 8), (1, 4)))
    query_weight = scatter_about(streams_of[5], (D, F), D ** -0.5, 0.0546875, ((0, 4), (1, 8)))
    keyval_weight = scatter_about(streams_of[6], (D, G), D ** -0.5, 0.0546875, ((0, 4),))
    out_weight = scatter_about(streams_of[7], (F, D), F ** -0.5, 0.078125, ((0, 8), (1, 4)))
    return {"layer_input": layer_input, "heads_output": heads_output, "query_cot": query_cot, "keyval_cot": keyval_cot, "output_cot": output_cot, "query_weight": query_weight, "keyval_weight": keyval_weight, "out_weight": out_weight}


def reference(layer_input, heads_output, query_cot, keyval_cot, output_cot, query_weight, keyval_weight, out_weight):
    input_grad = jnp.dot(query_cot, query_weight.T, preferred_element_type=jnp.float32)
    input_grad = input_grad + jnp.dot(keyval_cot, keyval_weight.T, preferred_element_type=jnp.float32)
    heads_grad = jnp.dot(output_cot, out_weight.T, preferred_element_type=jnp.float32)
    query_wgrad = jnp.dot(layer_input.T, query_cot, preferred_element_type=jnp.float32)
    keyval_wgrad = jnp.dot(layer_input.T, keyval_cot, preferred_element_type=jnp.float32)
    out_wgrad = jnp.dot(heads_output.T, output_cot, preferred_element_type=jnp.float32)
    return (input_grad.astype(jnp.bfloat16), heads_grad.astype(jnp.bfloat16), query_wgrad.astype(jnp.bfloat16), keyval_wgrad.astype(jnp.bfloat16), out_wgrad.astype(jnp.bfloat16))
```

```python
import jax
import jax.numpy as jnp
from jax import lax
from jax.sharding import PartitionSpec as P


def contract_last(left, right):
    return lax.dot_general(
        left, right, (((1,), (1,)), ((), ())), preferred_element_type=jnp.float32
    )


def contract_first(left, right):
    return lax.dot_general(
        left, right, (((0,), (0,)), ((), ())), preferred_element_type=jnp.float32
    )


def shards(
    layer_input,
    heads_output,
    query_cot,
    keyval_cot,
    output_cot,
    query_weight,
    keyval_weight,
    out_weight,
):
    query_all, heads_all = (
        lax.all_gather(query_cot, "row", axis=0, tiled=True),
        lax.all_gather(heads_output, "row", axis=0, tiled=True),
    )
    output_all, input_all = (
        lax.all_gather(output_cot, "col", axis=0, tiled=True),
        lax.all_gather(layer_input, "col", axis=0, tiled=True),
    )
    keyval_term = contract_last(keyval_cot, keyval_weight)
    picked = query_all
    summed = (
        lax.psum_scatter(
            contract_last(picked, query_weight), "col", scatter_dimension=0, tiled=True
        )
        + keyval_term
    )
    input_grad = summed.astype(jnp.bfloat16)
    picked = output_all
    heads_sum = lax.psum_scatter(
        contract_last(picked, out_weight), "row", scatter_dimension=0, tiled=True
    )
    heads_grad = heads_sum.astype(jnp.bfloat16)
    query_wgrad = contract_first(input_all, query_all).astype(jnp.bfloat16)
    out_wgrad = contract_first(heads_all, output_all).astype(jnp.bfloat16)
    keyval_all = lax.all_gather(keyval_cot, "col", axis=0, tiled=True)
    keyval_wgrad = contract_first(input_all, keyval_all).astype(jnp.bfloat16)
    return (input_grad, heads_grad, query_wgrad, keyval_wgrad, out_wgrad)


def solution(mesh):
    in_specs = (
        P("col", "row"),
        P("row", "col"),
        P("row", "col"),
        P("col", None),
        P("col", "row"),
        P("row", "col"),
        P("row", None),
        P("col", "row"),
    )
    out_specs = (P("col", "row"), P("row", "col"), P("row", "col"), P("row", None), P("col", "row"))
    return jax.shard_map(shards, mesh=mesh, in_specs=in_specs, out_specs=out_specs, check_vma=False)
```

```python
import functools

import jax
import jax.numpy as jnp
from jax import lax
from jax.experimental import pallas as pl
from jax.experimental.pallas import tpu as pltpu
from jax.sharding import PartitionSpec as P

F32, BF16 = jnp.float32, jnp.bfloat16


def contract_last(left, right):
    return lax.dot_general(
        left, right, (((1,), (1,)), ((), ())), preferred_element_type=jnp.float32
    )


def contract_first(left, right):
    return lax.dot_general(
        left, right, (((0,), (0,)), ((), ())), preferred_element_type=jnp.float32
    )


def shards(
    layer_input,
    heads_output,
    query_cot,
    keyval_cot,
    output_cot,
    query_weight,
    keyval_weight,
    out_weight,
):
    query_all, heads_all = (
        lax.all_gather(query_cot, "row", axis=0, tiled=True),
        lax.all_gather(heads_output, "row", axis=0, tiled=True),
    )
    output_all, input_all = (
        lax.all_gather(output_cot, "col", axis=0, tiled=True),
        lax.all_gather(layer_input, "col", axis=0, tiled=True),
    )
    keyval_term = contract_last(keyval_cot, keyval_weight)
    picked = query_all
    summed = (
        lax.psum_scatter(
            contract_last(picked, query_weight), "col", scatter_dimension=0, tiled=True
        )
        + keyval_term
    )
    input_grad = summed.astype(jnp.bfloat16)
    picked = output_all
    heads_sum = lax.psum_scatter(
        contract_last(picked, out_weight), "row", scatter_dimension=0, tiled=True
    )
    heads_grad = heads_sum.astype(jnp.bfloat16)
    query_wgrad = contract_first(input_all, query_all).astype(jnp.bfloat16)
    out_wgrad = contract_first(heads_all, output_all).astype(jnp.bfloat16)
    keyval_all = lax.all_gather(keyval_cot, "col", axis=0, tiled=True)
    keyval_wgrad = contract_first(input_all, keyval_all).astype(jnp.bfloat16)
    return (input_grad, heads_grad, query_wgrad, keyval_wgrad, out_wgrad)


def remote(src, dst, send, recv, device):
    return pltpu.make_async_remote_copy(
        src_ref=src, dst_ref=dst, send_sem=send, recv_sem=recv,
        device_id=device, device_id_type=pl.DeviceIdType.MESH,
    )


CHUNKS = 6
COPIES = 8


class PlaneGather:
    def __init__(self, src, whole, local, send, recv, place):
        self.src, self.whole, self.local = src, whole, local
        self.send, self.recv = send, recv
        self.z, self.col, self.xn, self.yn, self.dn, self.sib, self.flip = place
        half = src.shape[0] // 2
        low, high = pl.ds(0, half), pl.ds(half, half)
        w = whole
        self.plan = [
            (None, None, self.xn), (None, None, self.yn), (None, None, self.sib),
            (self.xn, low, self.yn), (self.yn, high, self.xn),
            (self.xn, None, self.sib), (self.yn, None, self.sib), (self.dn, None, self.sib),
        ]
        self.lands = [
            (self.xn, None), (self.yn, None), (self.sib, None),
            (self.dn, low), (self.dn, high),
            (self.flip(self.xn), None), (self.flip(self.yn), None), (self.flip(self.dn), None),
        ]

    def at(self, block, rows):
        return self.whole.at[block] if rows is None else self.whole.at[block, rows]

    def copy(self, i):
        block, rows, to = self.plan[i]
        src = self.src if block is None else self.at(block, rows)
        dst = self.at(self.col if block is None else block, rows)
        return remote(src, dst, self.send.at[i], self.recv.at[i], (self.z, to))

    def own(self):
        return pltpu.make_async_copy(self.src, self.whole.at[self.col], self.local)

    def arrive(self, i):
        ref = self.at(*self.lands[i])
        remote(ref, ref, self.send.at[i], self.recv.at[i], (self.z, self.xn)).wait_recv()

    def begin(self):
        self.own().start()
        for i in (0, 1, 2):
            self.copy(i).start()

    def forward(self):
        self.arrive(0)
        self.copy(3).start()
        self.copy(5).start()
        self.arrive(1)
        self.copy(4).start()
        self.copy(6).start()

    def diagonal(self):
        self.arrive(3)
        self.arrive(4)
        self.copy(7).start()

    def finish(self):
        self.own().wait()
        for i in (2, 5, 6, 7):
            self.arrive(i)

    def sent(self):
        for i in range(COPIES):
            self.copy(i).wait_send()


class LineGather:
    def __init__(self, src, whole, local, up, down, recv, z, col, n):
        self.src, self.whole, self.local = src, whole, local
        self.up, self.down, self.recv = up, down, recv
        self.z, self.col, self.n = z, col, n

    def copy(self, block, step, direction):
        src = self.src if step == 0 else self.whole.at[block]
        sems = self.up if direction > 0 else self.down
        return remote(src, self.whole.at[block], sems.at[step], self.recv.at[block],
                      (self.z + direction, self.col))

    def own(self):
        return pltpu.make_async_copy(self.src, self.whole.at[self.z], self.local)

    def arrive(self, block):
        ref = self.whole.at[block]
        remote(ref, ref, self.up.at[0], self.recv.at[block], (self.z, self.col)).wait_recv()

    def sends(self, k, act):
        z, n = self.z, self.n

        @pl.when((z < n - 1) & (z - k >= 0))
        def _():
            act(self.copy(z - k, k, 1))

        @pl.when((z > 0) & (z + k <= n - 1))
        def _():
            act(self.copy(z + k, k, -1))

    def begin(self):
        self.own().start()
        self.sends(0, lambda c: c.start())

    def step(self, k):
        z, n = self.z, self.n

        @pl.when(z - k >= 0)
        def _():
            self.arrive(z - k)

            @pl.when(z < n - 1)
            def _():
                self.copy(z - k, k, 1).start()

        @pl.when(z + k <= n - 1)
        def _():
            self.arrive(z + k)

            @pl.when(z > 0)
            def _():
                self.copy(z + k, k, -1).start()

    def sent(self):
        for k in range(self.n - 1):
            self.sends(k, lambda c: c.wait_send())


def kernel(
    n,
    x, ho, qc, kc, oc, qw, kw, ow,
    ig, hg, qg, kg, og,
    x_all, h_all, q_all, k_all, o_all, qv, kv, ov,
    out0, sum0, in1, in2, hsum, hup, hdown, qs, ks, os,
    local, plane_send, plane_recv, line_up, line_down, line_recv,
    send0, recv0, send1, recv1, send2, recv2,
    hup_send, hup_recv, hdown_send, hdown_recv, store,
):
    z, col = lax.axis_index("row"), lax.axis_index("col")
    core, cx, cy = col % 2, (col // 2) % 2, col // 4
    ox, oy, ocore = 1 - cx, 1 - cy, 1 - core
    xn, yn = cy * 4 + ox * 2 + core, oy * 4 + cx * 2 + core
    dn, sib = oy * 4 + ox * 2 + core, cy * 4 + cx * 2 + ocore

    def flip(block):
        return block + 1 - 2 * core

    place = (z, col, xn, yn, dn, sib, flip)
    width = qw.shape[0] // CHUNKS

    loads = [pltpu.make_async_copy(a, b, local.at[5 + i])
             for i, (a, b) in enumerate(((qw, qv), (kw, kv), (ow, ov)))]
    for load in loads:
        load.start()

    barrier = pltpu.get_barrier_semaphore()
    for to in (xn, yn, sib):
        pl.semaphore_signal(barrier, inc=1, device_id=(z, to), device_id_type=pl.DeviceIdType.MESH)

    @pl.when(z > 0)
    def _():
        pl.semaphore_signal(barrier, inc=1, device_id=(z - 1, col), device_id_type=pl.DeviceIdType.MESH)

    @pl.when(z < n - 1)
    def _():
        pl.semaphore_signal(barrier, inc=1, device_id=(z + 1, col), device_id_type=pl.DeviceIdType.MESH)

    pl.semaphore_wait(barrier, 3 + jnp.where(z > 0, 1, 0) + jnp.where(z < n - 1, 1, 0))

    gx = PlaneGather(x, x_all, local.at[0], plane_send.at[0], plane_recv.at[0], place)
    go = PlaneGather(oc, o_all, local.at[1], plane_send.at[1], plane_recv.at[1], place)
    gk = PlaneGather(kc, k_all, local.at[2], plane_send.at[2], plane_recv.at[2], place)
    gq = LineGather(qc, q_all, local.at[3], line_up.at[0], line_down.at[0], line_recv.at[0], z, col, n)
    gh = LineGather(ho, h_all, local.at[4], line_up.at[1], line_down.at[1], line_recv.at[1], z, col, n)

    def partial(j, which):
        rows = q_all[:, pl.ds(which, 1)].reshape(-1, q_all.shape[-1])
        part = contract_last(rows, qv[pl.ds(j * width, width), :])
        return part.reshape(2, 2, -1, width)

    def move0(j):
        return remote(out0.at[j % 2], sum0.at[j], send0.at[j], recv0.at[j], (z, sib))

    def move1(j):
        if j % 2 == 0:
            return remote(sum0.at[j, :, ox], in1.at[j], send1.at[j], recv1.at[j], (z, xn))
        return remote(sum0.at[j, oy], in1.at[j], send1.at[j], recv1.at[j], (z, yn))

    def move2(j):
        if j % 2 == 0:
            return remote(sum0.at[j, oy, cx], in2.at[j], send2.at[j], recv2.at[j], (z, yn))
        return remote(sum0.at[j, cy, ox], in2.at[j], send2.at[j], recv2.at[j], (z, xn))

    def stage0(j):
        if j >= 2:
            move0(j - 2).wait_send()
        out0[j % 2] = partial(j, ocore)
        move0(j).start()

    def stage1(j):
        own = partial(j, core)
        move0(j).wait_recv()
        sum0[j] += own
        move1(j).start()

    def stage2(j):
        move1(j).wait_recv()
        if j % 2 == 0:
            sum0[j, oy, cx] += in1[j, oy]
            move2(j).start()
            sum0[j, cy, cx] += in1[j, cy]
        else:
            sum0[j, cy, ox] += in1[j, ox]
            move2(j).start()
            sum0[j, cy, cx] += in1[j, cx]

    def stage3(j):
        term = contract_last(k_all[col], kv[pl.ds(j * width, width), :])
        move2(j).wait_recv()
        total = sum0[j, cy, cx] + in2[j] + term
        ig[:, j * width:(j + 1) * width] = total.astype(BF16)

    def heads_product():
        @pl.loop(0, n)
        def _(b):
            rows = o_all[pl.ds(2 * b, 2)].reshape(-1, o_all.shape[-1])
            hsum[b] = contract_last(rows, ov[...])

    def hmove(t, direction):
        if direction > 0:
            return remote(hsum.at[t], hup.at[t], hup_send.at[t], hup_recv.at[t], (z + 1, col))
        return remote(hsum.at[t], hdown.at[t], hdown_send.at[t], hdown_recv.at[t], (z - 1, col))

    def heads_step(p):
        up = n - 1 - p + z

        @pl.when(z <= p)
        def _():
            @pl.when(z > 0)
            def _():
                hmove(up, 1).wait_recv()
                hsum[up] += hup[up]

            hmove(up, 1).start()

        down = p - (n - 1 - z)

        @pl.when(n - 1 - z <= p)
        def _():
            @pl.when(z < n - 1)
            def _():
                hmove(down, -1).wait_recv()
                hsum[down] += hdown[down]

            hmove(down, -1).start()

    def heads_last():
        @pl.when(z > 0)
        def _():
            hmove(z, 1).wait_recv()
            hsum[z] += hup[z]

        @pl.when(z < n - 1)
        def _():
            hmove(z, -1).wait_recv()
            hsum[z] += hdown[z]

        hg[...] = hsum[z].astype(BF16)
        for t in range(n):
            @pl.when(z < t)
            def _():
                hmove(t, 1).wait_send()

            @pl.when(z > t)
            def _():
                hmove(t, -1).wait_send()

    tile = 256

    def put(slots, slot, target, sem):
        return pltpu.make_async_copy(slots.at[slot], target, sem.at[slot])

    def layer_weights(first, last):
        @pl.loop(first, last)
        def _(i):
            cols = pl.ds(pl.multiple_of(i * tile, tile), tile)
            slot = lax.rem(i, 2)

            @pl.when(i >= 2)
            def _():
                put(qs, slot, qg.at[cols], store.at[0]).wait()
                put(ks, slot, kg.at[cols], store.at[1]).wait()

            rows = x_all[:, :, cols].reshape(-1, tile)
            qs[slot] = contract_first(rows, q_all[...].reshape(-1, q_all.shape[-1])).astype(BF16)
            put(qs, slot, qg.at[cols], store.at[0]).start()
            ks[slot] = contract_first(rows, k_all[...].reshape(-1, k_all.shape[-1])).astype(BF16)
            put(ks, slot, kg.at[cols], store.at[1]).start()

    def layer_weights_done():
        for slot in range(2):
            put(qs, slot, qg.at[pl.ds(0, tile)], store.at[0]).wait()
            put(ks, slot, kg.at[pl.ds(0, tile)], store.at[1]).wait()

    pieces = o_all.shape[-1] // 1024
    out_tiles = (h_all.shape[-1] // tile) * pieces

    def out_target(i):
        cols = pl.ds(pl.multiple_of((i // pieces) * tile, tile), tile)
        wide = pl.ds(pl.multiple_of((i % pieces) * 1024, 1024), 1024)
        return cols, wide

    def out_weights():
        @pl.loop(0, out_tiles)
        def _(i):
            cols, wide = out_target(i)
            slot = lax.rem(i, 2)

            @pl.when(i >= 2)
            def _():
                put(os, slot, og.at[cols, wide], store.at[2]).wait()

            rows = h_all[:, :, :, cols].reshape(-1, tile)
            os[slot] = contract_first(rows, o_all[:, :, wide].reshape(-1, 1024)).astype(BF16)
            put(os, slot, og.at[cols, wide], store.at[2]).start()

        for slot in range(2):
            put(os, slot, og.at[pl.ds(0, tile), pl.ds(0, 1024)], store.at[2]).wait()

    tiles = qw.shape[0] // tile

    gq.begin()
    go.begin()
    gk.begin()
    gq.step(1)
    gq.step(2)
    gh.begin()
    go.forward()
    gx.begin()
    gk.forward()
    gq.step(3)
    gq.own().wait()
    for load in loads:
        load.wait()
    stage0(0)
    go.diagonal()
    gk.diagonal()
    stage0(1)
    stage1(0)
    go.finish()
    heads_product()
    heads_step(0)
    gh.step(1)
    stage0(2)
    stage1(1)
    gk.finish()
    gx.forward()
    gh.step(2)
    stage2(0)
    stage0(3)
    stage1(2)
    heads_step(1)
    gx.diagonal()
    stage2(1)
    stage3(0)
    stage0(4)
    stage1(3)
    gh.step(3)
    gh.own().wait()
    stage2(2)
    stage3(1)
    stage0(5)
    stage1(4)
    stage1(5)
    heads_step(2)
    out_weights()
    stage2(3)
    stage3(2)
    gx.finish()
    layer_weights(0, tiles // 2)
    stage2(4)
    stage3(3)
    stage2(5)
    layer_weights(tiles // 2, tiles)
    heads_last()
    stage3(4)
    stage3(5)
    layer_weights_done()
    for g in (gx, go, gk, gq, gh):
        g.sent()
    for j in range(CHUNKS):
        if j >= CHUNKS - 2:
            move0(j).wait_send()
        move1(j).wait_send()
        move2(j).wait_send()


def fused(x, ho, qc, kc, oc, qw, kw, ow):
    n, m = lax.axis_size("row"), lax.axis_size("col")
    tokens, features = x.shape
    heads, groups = qw.shape[1], kw.shape[1]
    width = features // CHUNKS
    split = (2, tokens, heads)
    dma = pltpu.SemaphoreType.DMA
    any_space = pl.BlockSpec(memory_space=pl.ANY)
    vmem = pl.BlockSpec(memory_space=pltpu.VMEM)
    s = jax.ShapeDtypeStruct
    return pl.pallas_call(
        functools.partial(kernel, n),
        out_shape=(
            s((tokens, features), BF16), s((2 * tokens, heads), BF16),
            s((features, heads), BF16), s((features, groups), BF16), s((heads, features), BF16),
        ),
        in_specs=[any_space] * 8,
        out_specs=(vmem, vmem, any_space, any_space, any_space),
        scratch_shapes=[
            pltpu.VMEM((m, tokens, features), BF16),
            pltpu.VMEM((n,) + split, BF16),
            pltpu.VMEM((n,) + split, BF16),
            pltpu.VMEM((m, tokens, groups), BF16),
            pltpu.VMEM((m, tokens, features), BF16),
            pltpu.VMEM(qw.shape, BF16),
            pltpu.VMEM(kw.shape, BF16),
            pltpu.VMEM(ow.shape, BF16),
            pltpu.VMEM((2, 2, 2, tokens, width), F32),
            pltpu.VMEM((CHUNKS, 2, 2, tokens, width), F32),
            pltpu.VMEM((CHUNKS, 2, tokens, width), F32),
            pltpu.VMEM((CHUNKS, tokens, width), F32),
            pltpu.VMEM((n, 2 * tokens, heads), F32),
            pltpu.VMEM((n, 2 * tokens, heads), F32),
            pltpu.VMEM((n, 2 * tokens, heads), F32),
            pltpu.VMEM((2, 256, heads), BF16),
            pltpu.VMEM((2, 256, groups), BF16),
            pltpu.VMEM((2, 256, 1024), BF16),
            dma((8,)), dma((3, COPIES)), dma((3, COPIES)),
            dma((2, n)), dma((2, n)), dma((2, n)),
            dma((CHUNKS,)), dma((CHUNKS,)), dma((CHUNKS,)),
            dma((CHUNKS,)), dma((CHUNKS,)), dma((CHUNKS,)),
            dma((n,)), dma((n,)), dma((n,)), dma((n,)), dma((3, 2)),
        ],
        compiler_params=pltpu.CompilerParams(
            collective_id=0, has_side_effects=True, vmem_limit_bytes=64 * 1024 * 1024 - 65536
        ),
        cost_estimate=pl.CostEstimate(flops=26 * 10**9, bytes_accessed=60 * 10**6, transcendentals=0),
    )(x, ho.reshape(split), qc.reshape(split), kc, oc, qw, kw, ow)


def solution(mesh):
    in_specs = (
        P("col", "row"),
        P("row", "col"),
        P("row", "col"),
        P("col", None),
        P("col", "row"),
        P("row", "col"),
        P("row", None),
        P("col", "row"),
    )
    out_specs = (P("col", "row"), P("row", "col"), P("row", "col"), P("row", None), P("col", "row"))
    body = fused if mesh.shape["row"] == 4 and mesh.shape["col"] == 8 else shards
    return jax.shard_map(body, mesh=mesh, in_specs=in_specs, out_specs=out_specs, check_vma=False)
```

```python
import functools

import jax
import jax.numpy as jnp
from jax import lax
from jax.experimental import pallas as pl
from jax.experimental.pallas import tpu as pltpu
from jax.sharding import PartitionSpec as P

F32, BF16 = jnp.float32, jnp.bfloat16


def contract_last(left, right):
    return lax.dot_general(
        left, right, (((1,), (1,)), ((), ())), preferred_element_type=jnp.float32
    )


def contract_first(left, right):
    return lax.dot_general(
        left, right, (((0,), (0,)), ((), ())), preferred_element_type=jnp.float32
    )


def shards(
    layer_input,
    heads_output,
    query_cot,
    keyval_cot,
    output_cot,
    query_weight,
    keyval_weight,
    out_weight,
):
    query_all, heads_all = (
        lax.all_gather(query_cot, "row", axis=0, tiled=True),
        lax.all_gather(heads_output, "row", axis=0, tiled=True),
    )
    output_all, input_all = (
        lax.all_gather(output_cot, "col", axis=0, tiled=True),
        lax.all_gather(layer_input, "col", axis=0, tiled=True),
    )
    keyval_term = contract_last(keyval_cot, keyval_weight)
    picked = query_all
    summed = (
        lax.psum_scatter(
            contract_last(picked, query_weight), "col", scatter_dimension=0, tiled=True
        )
        + keyval_term
    )
    input_grad = summed.astype(jnp.bfloat16)
    picked = output_all
    heads_sum = lax.psum_scatter(
        contract_last(picked, out_weight), "row", scatter_dimension=0, tiled=True
    )
    heads_grad = heads_sum.astype(jnp.bfloat16)
    query_wgrad = contract_first(input_all, query_all).astype(jnp.bfloat16)
    out_wgrad = contract_first(heads_all, output_all).astype(jnp.bfloat16)
    keyval_all = lax.all_gather(keyval_cot, "col", axis=0, tiled=True)
    keyval_wgrad = contract_first(input_all, keyval_all).astype(jnp.bfloat16)
    return (input_grad, heads_grad, query_wgrad, keyval_wgrad, out_wgrad)


def remote(src, dst, send, recv, device):
    return pltpu.make_async_remote_copy(
        src_ref=src, dst_ref=dst, send_sem=send, recv_sem=recv,
        device_id=device, device_id_type=pl.DeviceIdType.MESH,
    )


CHUNKS = 6
COPIES = 8


class PlaneGather:
    def __init__(self, src, whole, local, send, recv, place):
        self.src, self.whole, self.local = src, whole, local
        self.send, self.recv = send, recv
        self.z, self.col, self.xn, self.yn, self.dn, self.sib, self.flip = place
        half = src.shape[0] // 2
        low, high = pl.ds(0, half), pl.ds(half, half)
        w = whole
        self.plan = [
            (None, None, self.xn), (None, None, self.yn), (None, None, self.sib),
            (self.xn, low, self.yn), (self.yn, high, self.xn),
            (self.xn, None, self.sib), (self.yn, None, self.sib), (self.dn, None, self.sib),
        ]
        self.lands = [
            (self.xn, None), (self.yn, None), (self.sib, None),
            (self.dn, low), (self.dn, high),
            (self.flip(self.xn), None), (self.flip(self.yn), None), (self.flip(self.dn), None),
        ]

    def at(self, block, rows):
        return self.whole.at[block] if rows is None else self.whole.at[block, rows]

    def copy(self, i):
        block, rows, to = self.plan[i]
        src = self.src if block is None else self.at(block, rows)
        dst = self.at(self.col if block is None else block, rows)
        return remote(src, dst, self.send.at[i], self.recv.at[i], (self.z, to))

    def own(self):
        return pltpu.make_async_copy(self.src, self.whole.at[self.col], self.local)

    def arrive(self, i):
        ref = self.at(*self.lands[i])
        remote(ref, ref, self.send.at[i], self.recv.at[i], (self.z, self.xn)).wait_recv()

    def begin(self):
        self.own().start()
        for i in (0, 1, 2):
            self.copy(i).start()

    def forward(self):
        self.arrive(0)
        self.copy(3).start()
        self.copy(5).start()
        self.arrive(1)
        self.copy(4).start()
        self.copy(6).start()

    def diagonal(self):
        self.arrive(3)
        self.arrive(4)
        self.copy(7).start()

    def finish(self):
        for i in (2, 5, 6, 7):
            self.arrive(i)

    def sent(self):
        for i in range(COPIES):
            self.copy(i).wait_send()


class LineGather:
    def __init__(self, src, whole, local, up, down, recv, z, col, n):
        self.src, self.whole, self.local = src, whole, local
        self.up, self.down, self.recv = up, down, recv
        self.z, self.col, self.n = z, col, n

    def copy(self, block, step, direction):
        src = self.src if step == 0 else self.whole.at[block]
        sems = self.up if direction > 0 else self.down
        return remote(src, self.whole.at[block], sems.at[step], self.recv.at[block],
                      (self.z + direction, self.col))

    def own(self):
        return pltpu.make_async_copy(self.src, self.whole.at[self.z], self.local)

    def arrive(self, block):
        ref = self.whole.at[block]
        remote(ref, ref, self.up.at[0], self.recv.at[block], (self.z, self.col)).wait_recv()

    def sends(self, k, act):
        z, n = self.z, self.n

        @pl.when((z < n - 1) & (z - k >= 0))
        def _():
            act(self.copy(z - k, k, 1))

        @pl.when((z > 0) & (z + k <= n - 1))
        def _():
            act(self.copy(z + k, k, -1))

    def begin(self):
        self.own().start()
        self.sends(0, lambda c: c.start())

    def step(self, k):
        z, n = self.z, self.n

        @pl.when(z - k >= 0)
        def _():
            self.arrive(z - k)

            @pl.when(z < n - 1)
            def _():
                self.copy(z - k, k, 1).start()

        @pl.when(z + k <= n - 1)
        def _():
            self.arrive(z + k)

            @pl.when(z > 0)
            def _():
                self.copy(z + k, k, -1).start()

    def sent(self):
        for k in range(self.n - 1):
            self.sends(k, lambda c: c.wait_send())


def kernel(
    n,
    x, ho, qc, kc, oc, qw, kw, ow,
    ig, hg, qg, kg, og,
    x_all, h_all, q_all, k_all, o_all, qv, kv, ov,
    out0, sum0, in1, in2, hsum, hup, hdown, qs, ks, os,
    local, plane_send, plane_recv, line_up, line_down, line_recv,
    send0, recv0, send1, recv1, send2, recv2,
    hup_send, hup_recv, hdown_send, hdown_recv, store,
):
    z, col = lax.axis_index("row"), lax.axis_index("col")
    core, cx, cy = col % 2, (col // 2) % 2, col // 4
    ox, oy, ocore = 1 - cx, 1 - cy, 1 - core
    xn, yn = cy * 4 + ox * 2 + core, oy * 4 + cx * 2 + core
    dn, sib = oy * 4 + ox * 2 + core, cy * 4 + cx * 2 + ocore

    def flip(block):
        return block + 1 - 2 * core

    place = (z, col, xn, yn, dn, sib, flip)
    width = qw.shape[0] // CHUNKS

    loads = [pltpu.make_async_copy(a, b, local.at[5 + i])
             for i, (a, b) in enumerate(((qw, qv), (kw, kv), (ow, ov)))]
    for load in loads:
        load.start()

    barrier = pltpu.get_barrier_semaphore()
    for to in (xn, yn, sib):
        pl.semaphore_signal(barrier, inc=1, device_id=(z, to), device_id_type=pl.DeviceIdType.MESH)

    @pl.when(z > 0)
    def _():
        pl.semaphore_signal(barrier, inc=1, device_id=(z - 1, col), device_id_type=pl.DeviceIdType.MESH)

    @pl.when(z < n - 1)
    def _():
        pl.semaphore_signal(barrier, inc=1, device_id=(z + 1, col), device_id_type=pl.DeviceIdType.MESH)

    pl.semaphore_wait(barrier, 3 + jnp.where(z > 0, 1, 0) + jnp.where(z < n - 1, 1, 0))

    gx = PlaneGather(x, x_all, local.at[0], plane_send.at[0], plane_recv.at[0], place)
    go = PlaneGather(oc, o_all, local.at[1], plane_send.at[1], plane_recv.at[1], place)
    gk = PlaneGather(kc, k_all, local.at[2], plane_send.at[2], plane_recv.at[2], place)
    gq = LineGather(qc, q_all, local.at[3], line_up.at[0], line_down.at[0], line_recv.at[0], z, col, n)
    gh = LineGather(ho, h_all, local.at[4], line_up.at[1], line_down.at[1], line_recv.at[1], z, col, n)

    def partial(j, which):
        rows = q_all[:, pl.ds(which, 1)].reshape(-1, q_all.shape[-1])
        part = contract_last(rows, qv[pl.ds(j * width, width), :])
        return part.reshape(2, 2, -1, width)

    def move0(j):
        return remote(out0.at[j % 2], sum0.at[j], send0.at[j], recv0.at[j], (z, sib))

    def move1(j):
        if j % 2 == 0:
            return remote(sum0.at[j, :, ox], in1.at[j], send1.at[j], recv1.at[j], (z, xn))
        return remote(sum0.at[j, oy], in1.at[j], send1.at[j], recv1.at[j], (z, yn))

    def move2(j):
        if j % 2 == 0:
            return remote(sum0.at[j, oy, cx], in2.at[j], send2.at[j], recv2.at[j], (z, yn))
        return remote(sum0.at[j, cy, ox], in2.at[j], send2.at[j], recv2.at[j], (z, xn))

    def stage0(j):
        if j >= 2:
            move0(j - 2).wait_send()
        out0[j % 2] = partial(j, ocore)
        move0(j).start()

    def stage1(j):
        own = partial(j, core)
        move0(j).wait_recv()
        sum0[j] += own
        move1(j).start()

    def stage2(j):
        move1(j).wait_recv()
        if j % 2 == 0:
            sum0[j, oy, cx] += in1[j, oy]
            move2(j).start()
            sum0[j, cy, cx] += in1[j, cy]
        else:
            sum0[j, cy, ox] += in1[j, ox]
            move2(j).start()
            sum0[j, cy, cx] += in1[j, cx]

    def stage3(j):
        term = contract_last(k_all[col], kv[pl.ds(j * width, width), :])
        move2(j).wait_recv()
        total = sum0[j, cy, cx] + in2[j] + term
        ig[:, j * width:(j + 1) * width] = total.astype(BF16)

    def heads_product():
        @pl.loop(0, n)
        def _(b):
            rows = o_all[pl.ds(2 * b, 2)].reshape(-1, o_all.shape[-1])
            hsum[b] = contract_last(rows, ov[...])

    def hmove(t, direction):
        if direction > 0:
            return remote(hsum.at[t], hup.at[t], hup_send.at[t], hup_recv.at[t], (z + 1, col))
        return remote(hsum.at[t], hdown.at[t], hdown_send.at[t], hdown_recv.at[t], (z - 1, col))

    def heads_step(p):
        up = n - 1 - p + z

        @pl.when(z <= p)
        def _():
            @pl.when(z > 0)
            def _():
                hmove(up, 1).wait_recv()
                hsum[up] += hup[up]

            hmove(up, 1).start()

        down = p - (n - 1 - z)

        @pl.when(n - 1 - z <= p)
        def _():
            @pl.when(z < n - 1)
            def _():
                hmove(down, -1).wait_recv()
                hsum[down] += hdown[down]

            hmove(down, -1).start()

    def heads_last():
        @pl.when(z > 0)
        def _():
            hmove(z, 1).wait_recv()
            hsum[z] += hup[z]

        @pl.when(z < n - 1)
        def _():
            hmove(z, -1).wait_recv()
            hsum[z] += hdown[z]

        hg[...] = hsum[z].astype(BF16)
        for t in range(n):
            @pl.when(z < t)
            def _():
                hmove(t, 1).wait_send()

            @pl.when(z > t)
            def _():
                hmove(t, -1).wait_send()

    tile = 256

    def put(slots, slot, target, sem):
        return pltpu.make_async_copy(slots.at[slot], target, sem.at[slot])

    def layer_weights(first, last):
        @pl.loop(first, last)
        def _(i):
            cols = pl.ds(pl.multiple_of(i * tile, tile), tile)
            slot = lax.rem(i, 2)

            @pl.when(i >= 2)
            def _():
                put(qs, slot, qg.at[cols], store.at[0]).wait()
                put(ks, slot, kg.at[cols], store.at[1]).wait()

            rows = x_all[:, :, cols].reshape(-1, tile)
            qs[slot] = contract_first(rows, q_all[...].reshape(-1, q_all.shape[-1])).astype(BF16)
            put(qs, slot, qg.at[cols], store.at[0]).start()
            ks[slot] = contract_first(rows, k_all[...].reshape(-1, k_all.shape[-1])).astype(BF16)
            put(ks, slot, kg.at[cols], store.at[1]).start()

    def layer_weights_done():
        for slot in range(2):
            put(qs, slot, qg.at[pl.ds(0, tile)], store.at[0]).wait()
            put(ks, slot, kg.at[pl.ds(0, tile)], store.at[1]).wait()

    pieces = o_all.shape[-1] // 1024
    out_tiles = (h_all.shape[-1] // tile) * pieces

    def out_target(i):
        cols = pl.ds(pl.multiple_of((i // pieces) * tile, tile), tile)
        wide = pl.ds(pl.multiple_of((i % pieces) * 1024, 1024), 1024)
        return cols, wide

    def out_weights():
        @pl.loop(0, out_tiles)
        def _(i):
            cols, wide = out_target(i)
            slot = lax.rem(i, 2)

            @pl.when(i >= 2)
            def _():
                put(os, slot, og.at[cols, wide], store.at[2]).wait()

            rows = h_all[:, :, :, cols].reshape(-1, tile)
            os[slot] = contract_first(rows, o_all[:, :, wide].reshape(-1, 1024)).astype(BF16)
            put(os, slot, og.at[cols, wide], store.at[2]).start()

        for slot in range(2):
            put(os, slot, og.at[pl.ds(0, tile), pl.ds(0, 1024)], store.at[2]).wait()

    tiles = qw.shape[0] // tile

    gq.begin()
    go.begin()
    gq.step(1)
    gq.step(2)
    gh.begin()
    go.forward()
    gx.begin()
    gk.begin()
    gq.step(3)
    gq.own().wait()
    go.own().wait()
    gx.own().wait()
    gk.own().wait()
    for load in loads:
        load.wait()
    stage0(0)
    go.diagonal()
    stage0(1)
    stage1(0)
    go.finish()
    heads_product()
    heads_step(0)
    gh.step(1)
    stage0(2)
    stage1(1)
    gx.forward()
    gk.forward()
    gh.step(2)
    stage2(0)
    stage0(3)
    stage1(2)
    heads_step(1)
    gx.diagonal()
    gk.diagonal()
    stage2(1)
    stage3(0)
    stage0(4)
    stage1(3)
    gh.step(3)
    gh.own().wait()
    stage2(2)
    stage3(1)
    stage0(5)
    stage1(4)
    stage1(5)
    heads_step(2)
    out_weights()
    stage2(3)
    stage3(2)
    gx.finish()
    gk.finish()
    layer_weights(0, tiles // 2)
    stage2(4)
    stage3(3)
    stage2(5)
    layer_weights(tiles // 2, tiles)
    heads_last()
    stage3(4)
    stage3(5)
    layer_weights_done()
    for g in (gx, go, gk, gq, gh):
        g.sent()
    for j in range(CHUNKS):
        if j >= CHUNKS - 2:
            move0(j).wait_send()
        move1(j).wait_send()
        move2(j).wait_send()


def fused(x, ho, qc, kc, oc, qw, kw, ow):
    n, m = lax.axis_size("row"), lax.axis_size("col")
    tokens, features = x.shape
    heads, groups = qw.shape[1], kw.shape[1]
    width = features // CHUNKS
    split = (2, tokens, heads)
    dma = pltpu.SemaphoreType.DMA
    any_space = pl.BlockSpec(memory_space=pl.ANY)
    vmem = pl.BlockSpec(memory_space=pltpu.VMEM)
    s = jax.ShapeDtypeStruct
    return pl.pallas_call(
        functools.partial(kernel, n),
        out_shape=(
            s((tokens, features), BF16), s((2 * tokens, heads), BF16),
            s((features, heads), BF16), s((features, groups), BF16), s((heads, features), BF16),
        ),
        in_specs=[any_space] * 8,
        out_specs=(vmem, vmem, any_space, any_space, any_space),
        scratch_shapes=[
            pltpu.VMEM((m, tokens, features), BF16),
            pltpu.VMEM((n,) + split, BF16),
            pltpu.VMEM((n,) + split, BF16),
            pltpu.VMEM((m, tokens, groups), BF16),
            pltpu.VMEM((m, tokens, features), BF16),
            pltpu.VMEM(qw.shape, BF16),
            pltpu.VMEM(kw.shape, BF16),
            pltpu.VMEM(ow.shape, BF16),
            pltpu.VMEM((2, 2, 2, tokens, width), F32),
            pltpu.VMEM((CHUNKS, 2, 2, tokens, width), F32),
            pltpu.VMEM((CHUNKS, 2, tokens, width), F32),
            pltpu.VMEM((CHUNKS, tokens, width), F32),
            pltpu.VMEM((n, 2 * tokens, heads), F32),
            pltpu.VMEM((n, 2 * tokens, heads), F32),
            pltpu.VMEM((n, 2 * tokens, heads), F32),
            pltpu.VMEM((2, 256, heads), BF16),
            pltpu.VMEM((2, 256, groups), BF16),
            pltpu.VMEM((2, 256, 1024), BF16),
            dma((8,)), dma((3, COPIES)), dma((3, COPIES)),
            dma((2, n)), dma((2, n)), dma((2, n)),
            dma((CHUNKS,)), dma((CHUNKS,)), dma((CHUNKS,)),
            dma((CHUNKS,)), dma((CHUNKS,)), dma((CHUNKS,)),
            dma((n,)), dma((n,)), dma((n,)), dma((n,)), dma((3, 2)),
        ],
        compiler_params=pltpu.CompilerParams(
            collective_id=0, has_side_effects=True, vmem_limit_bytes=64 * 1024 * 1024 - 65536
        ),
        cost_estimate=pl.CostEstimate(flops=26 * 10**9, bytes_accessed=60 * 10**6, transcendentals=0),
    )(x, ho.reshape(split), qc.reshape(split), kc, oc, qw, kw, ow)


def solution(mesh):
    in_specs = (
        P("col", "row"),
        P("row", "col"),
        P("row", "col"),
        P("col", None),
        P("col", "row"),
        P("row", "col"),
        P("row", None),
        P("col", "row"),
    )
    out_specs = (P("col", "row"), P("row", "col"), P("row", "col"), P("row", None), P("col", "row"))
    body = fused if mesh.shape["row"] == 4 and mesh.shape["col"] == 8 else shards
    return jax.shard_map(body, mesh=mesh, in_specs=in_specs, out_specs=out_specs, check_vma=False)
```
